512 devices in a mesh: fsdp: 64 (over z, x), tp: 8 (over y, core).
Axes of the slice: x: 4, y: 4, z: 16, core: 2. Of those that a mesh axis runs over, the one named last changes fastest.
Arguments:
- momentum: float32 [8192, 14336], P('fsdp', 'tp'), may hold values from -45 to 45, as said below
- gradient: bfloat16 [8192, 14336], P('fsdp', 'tp'), may hold values from -6 to 6
- right_basis: float32 [14336, 512], P(('tp', 'fsdp')), may hold values from -0.046875 to 0.046875
Outputs:
- new_momentum: float32 [8192, 14336], P('fsdp', 'tp')
- new_basis: float32 [14336, 512], P(('tp', 'fsdp'))
- update: bfloat16 [8192, 14336], P('fsdp', 'tp')
The draws below stay inside these ranges and needn't reach their ends.
Inputs may be any that keep to these rules, and one draw needn't show every extreme that they name: Entries of momentum have magnitudes that vary by row and by column.
All inputs are finite; a program needn't handle non-finite values.
Results may differ from the reference program's by a relative error of at most 0.001.
Values sent between devices are 32-bit elements; how exact they have to be, the bound alone decides.
A program may use at most 64 MiB of HBM per device.

```python
import math
import jax
import jax.numpy as jnp
from jax import lax

ROWS = 8192
COLS = 14336
RANK = 512


def draw_momentum(key, part):
    key = jax.random.fold_in(key, 11)
    first, second, third = jax.random.split(key, 3)
    row_scale = jnp.exp(jax.random.uniform(second, (ROWS, 1), jnp.float32, math.log(0.3), math.log(3.0)))
    col_scale = jnp.exp(jax.random.uniform(third, (1, COLS), jnp.float32, math.log(0.3), math.log(3.0)))
    base = jnp.clip(jax.random.normal(first, (ROWS, COLS), jnp.float32), -5.0, 5.0)
    return (base * row_scale * col_scale).astype(jnp.float32)


def block_scale(own_key, dims, shards, low, top_value):
    def one(axis_at, parts):
        steps = jax.random.uniform(jax.random.fold_in(jax.random.fold_in(own_key, 6), axis_at), (parts,), jnp.float32, low / len(shards), top_value / len(shards))
        return jnp.repeat(jnp.exp(steps), dims[axis_at] // parts).reshape((-1,) + (1,) * (len(dims) - axis_at - 1))

    level = one(*shards[0])
    for cut in shards[1:]:
        level = level * one(*cut)
    return level


def scatter_about(stream_key, dims, deviation, bound, pieces=(), held_as=jnp.bfloat16):
    gain = block_scale(stream_key, dims, pieces, -0.22, 0.18) if pieces else 1.0
    result = jax.random.normal(stream_key, dims, jnp.float32) * deviation * gain
    return jnp.minimum(jnp.maximum(result, -bound), bound).astype(held_as)


def setup_inputs(seed: int = 0) -> dict:
    key_of = jax.random.split(jax.random.key(seed), 4)
    return {
        "momentum": draw_momentum(jax.random.fold_in(key_of[3], 71), 0),
        "gradient": scatter_about(key_of[1], (ROWS, COLS), 1.0, 6.0, ((0, 64), (1, 8))),
        "right_basis": scatter_about(key_of[2], (COLS, RANK), COLS ** -0.5, 0.046875, ((0, 512),), jnp.float32),
    }


def reference(momentum, gradient, right_basis):
    high = lax.Precision.HIGHEST
    blended = momentum + gradient.astype(jnp.float32)
    left = jnp.dot(blended.astype(jnp.float32), right_basis.astype(jnp.float32), precision=high, preferred_element_type=jnp.float32)
    gram = jnp.dot(left.T.astype(jnp.float32), left.astype(jnp.float32), precision=high, preferred_element_type=jnp.float32)
    lower = jnp.linalg.cholesky(gram)
    ortho = jax.scipy.linalg.solve_triangular(lower, left.T, lower=True).T
    right = jnp.dot(blended.T.astype(jnp.float32), ortho.astype(jnp.float32), precision=high, preferred_element_type=jnp.float32)
    new_momentum = blended - 0.1 * jnp.dot(ortho.astype(jnp.float32), right.T.astype(jnp.float32), precision=high, preferred_element_type=jnp.float32)
    squares = lax.optimization_barrier(jnp.sum(right * right, axis=0))
    new_basis = right / (jnp.sqrt(squares) + 1e-06)
    factor = jnp.sqrt(jnp.float32(ROWS) * jnp.float32(COLS) / jnp.float32(RANK))
    update = (factor * jnp.dot(ortho.astype(jnp.float32), new_basis.T.astype(jnp.float32), precision=high, preferred_element_type=jnp.float32)).astype(jnp.bfloat16)
    return (new_momentum, new_basis, update)
```

```python
import functools

import jax
import jax.numpy as jnp
from jax import lax
from jax.experimental import pallas as pl
from jax.experimental.pallas import tpu as pltpu
from jax.sharding import PartitionSpec as P

ROWS = 8192
COLS = 14336
RANK = 512
MESH = pl.DeviceIdType.MESH
LANE = 128
NX = 4
VMEM = pl.BlockSpec(memory_space=pltpu.VMEM)
F32 = jnp.float32
BF16 = jnp.bfloat16
NN = (((1,), (0,)), ((), ()))
TN = (((0,), (0,)), ((), ()))
NT = (((1,), (1,)), ((), ()))


def split2(v):
    hi = v.astype(BF16)
    return hi, (v - hi.astype(F32)).astype(BF16)


def dot3(a, b, dims):
    ah, al = a if isinstance(a, tuple) else split2(a)
    bh, bl = b if isinstance(b, tuple) else split2(b)
    d = functools.partial(lax.dot_general, dimension_numbers=dims, preferred_element_type=F32)
    return d(ah, bh) + (d(ah, bl) + d(al, bh))


def copy_to(src, dst, send, recv, where):
    return pltpu.make_async_remote_copy(
        src_ref=src, dst_ref=dst, send_sem=send, recv_sem=recv, device_id=where, device_id_type=MESH
    )


def greet(peers):
    barrier = pltpu.get_barrier_semaphore()
    for peer in peers:
        pl.semaphore_signal(barrier, inc=1, device_id=peer, device_id_type=MESH)
    pl.semaphore_wait(barrier, len(peers))


class Place:
    def __init__(self, nz):
        me = lax.axis_index("fsdp")
        self.nz = nz
        self.z = me // NX
        self.x = lax.rem(me, NX)

    def zat(self, d):
        return lax.rem(self.z + (d + self.nz), self.nz)

    def xat(self, d):
        return lax.rem(self.x + (d + NX), NX)

    def dev(self, dz, dx):
        return {"fsdp": self.zat(dz) * NX + self.xat(dx)}

    def ring(self):
        return [self.dev(1, 0), self.dev(-1, 0), self.dev(0, 1), self.dev(0, -1)]


class Cuts:
    def __init__(self, c):
        self.c = c
        self.a = (c * 9 // 14) // 8 * 8
        self.b = c - self.a
        self.a0 = (self.a // 2 + 7) // 8 * 8
        self.b0 = (self.b // 2 + 7) // 8 * 8
        self.A = (pl.ds(0, self.a), pl.ds(0, self.a0), pl.ds(self.a0, self.a - self.a0))
        self.B = (
            pl.ds(self.a, self.b),
            pl.ds(self.a, self.b0),
            pl.ds(self.a + self.b0, self.b - self.b0),
        )


AG_SEMS = 6


def ag_sems(nz):
    h = nz // 2
    return [
        pltpu.SemaphoreType.DMA((2, h + 1)),
        pltpu.SemaphoreType.DMA((2, h + 1)),
        pltpu.SemaphoreType.DMA((2, h + 1)),
        pltpu.SemaphoreType.DMA((2, h + 1)),
        pltpu.SemaphoreType.DMA((2, 2, h + 1)),
        pltpu.SemaphoreType.DMA((2, 2, h + 1)),
        pltpu.SemaphoreType.DMA((2, 2, h + 1)),
        pltpu.SemaphoreType.DMA((2, 2, h + 1)),
        pltpu.SemaphoreType.DMA((2, 2)),
        pltpu.SemaphoreType.DMA((2, 2)),
    ]


class Gather:
    def __init__(self, place, out, sems):
        self.p, self.out = place, out
        self.cut = Cuts(out.shape[2])
        self.h = place.nz // 2
        (self.za_s, self.za_r, self.zb_s, self.zb_r, self.xa_s, self.xa_r, self.xh_s, self.xh_r,
         self.xb_s, self.xb_r) = sems

    def za(self, d, s):
        sign = 1 - 2 * d
        src = self.p.zat(-sign * (s - 1))
        rows = self.cut.A[0]
        ref = self.out.at[src, self.p.x, rows, :]
        return copy_to(ref, ref, self.za_s.at[d, s], self.za_r.at[d, s], self.p.dev(sign, 0))

    def za_half(self, d):
        sign = 1 - 2 * d
        src = self.p.zat(-sign * (self.h - 1))
        ref = self.out.at[src, self.p.x, self.cut.A[1 + d], :]
        return copy_to(ref, ref, self.za_s.at[d, self.h], self.za_r.at[d, self.h], self.p.dev(sign, 0))

    def zb(self, d, s):
        sign = 1 - 2 * d
        src = self.p.zat(-sign * (s - 1))
        ref = self.out.at[src, :, self.cut.B[0], :]
        return copy_to(ref, ref, self.zb_s.at[d, s], self.zb_r.at[d, s], self.p.dev(sign, 0))

    def zb_half(self, d):
        sign = 1 - 2 * d
        src = self.p.zat(-sign * (self.h - 1))
        ref = self.out.at[src, pl.ds(d * (NX // 2), NX // 2), self.cut.B[0], :]
        return copy_to(ref, ref, self.zb_s.at[d, self.h], self.zb_r.at[d, self.h], self.p.dev(sign, 0))

    def xa(self, d, g, s):
        src = self.p.zat((2 * g - 1) * s)
        ref = self.out.at[src, self.p.x, self.cut.A[0], :]
        return copy_to(ref, ref, self.xa_s.at[d, g, s], self.xa_r.at[d, g, s], self.p.dev(0, 1 - 2 * d))

    def xh(self, d, g, s):
        sign = 1 - 2 * d
        src = self.p.zat((2 * g - 1) * s)
        ref = self.out.at[src, self.p.xat(-sign), self.cut.A[1 + d], :]
        return copy_to(ref, ref, self.xh_s.at[d, g, s], self.xh_r.at[d, g, s], self.p.dev(0, sign))

    def xb(self, d):
        ref = self.out.at[self.p.z, self.p.x, self.cut.B[0], :]
        return copy_to(ref, ref, self.xb_s.at[0, d], self.xb_r.at[0, d], self.p.dev(0, 1 - 2 * d))

    def xbh(self, d):
        sign = 1 - 2 * d
        ref = self.out.at[self.p.z, self.p.xat(-sign), self.cut.B[1 + d], :]
        return copy_to(ref, ref, self.xb_s.at[1, d], self.xb_r.at[1, d], self.p.dev(0, sign))

    def begin(self):
        for d in (0, 1):
            self.xb(d).start()
            self.za(d, 1).start()
        for d in (0, 1):
            self.xa(d, 0, 0).start()
        for d in (0, 1):
            self.xb(d).wait_recv()
            self.xbh(d).start()
        for d in (0, 1):
            self.xbh(d).wait_recv()
        for d in (0, 1):
            self.zb(d, 1).start()

    def onward(self, g, s):
        for d in (0, 1):
            self.xa(d, g, s).wait_recv()
            self.xh(d, g, s).start()

    def step(self, s):
        for g in (0, 1):
            self.za(g, s).wait_recv()
            self.za(g, s + 1).start()
        for g in (0, 1):
            for d in (0, 1):
                self.xa(d, g, s).start()
        for g in (0, 1):
            self.zb(g, s).wait_recv()
            self.zb(g, s + 1).start()

    def finish(self):
        h = self.h
        s = h - 1
        for g in (0, 1):
            self.za(g, s).wait_recv()
            self.za_half(g).start()
        for g in (0, 1):
            for d in (0, 1):
                self.xa(d, g, s).start()
        for g in (0, 1):
            self.zb(g, s).wait_recv()
            self.zb_half(g).start()
        self.onward(0, s - 1)
        self.onward(1, s - 1)
        for g in (0, 1):
            self.za_half(g).wait_recv()
        for d in (0, 1):
            self.xa(d, 0, h).start()
        self.onward(0, s)
        self.onward(1, s)
        self.onward(0, h)
        for g in (0, 1):
            self.zb_half(g).wait_recv()
        for d in (0, 1):
            self.xh(d, 0, 0).wait()
            self.xh(d, 0, h).wait()
            self.xa(d, 0, 0).wait_send()
            self.xa(d, 0, h).wait_send()
            self.xb(d).wait_send()
            self.xbh(d).wait_send()
            self.za_half(d).wait_send()
            self.zb_half(d).wait_send()

        def drain(i, _):
            for d in (0, 1):
                self.za(d, i).wait_send()
                self.zb(d, i).wait_send()
                for g in (0, 1):
                    self.xa(d, g, i).wait_send()
                    self.xh(d, g, i).wait()
            return _

        lax.fori_loop(1, h, drain, 0)

    def run(self):
        self.begin()
        self.step(1)
        self.onward(0, 0)

        def body(s, _):
            self.step(s)
            self.onward(0, s - 1)
            self.onward(1, s - 1)
            return _

        lax.fori_loop(2, self.h - 1, body, 0)
        self.finish()


def ag_kernel(nz, own_ref, out_ref, *sems):
    place = Place(nz)
    out_ref[place.z, place.x] = own_ref[...]
    greet(place.ring())
    Gather(place, out_ref, sems).run()


def all_gather(own, nz, cid):
    c = own.shape[0]
    return pl.pallas_call(
        functools.partial(ag_kernel, nz),
        out_shape=jax.ShapeDtypeStruct((nz, NX, c, LANE), F32),
        in_specs=[VMEM],
        out_specs=VMEM,
        scratch_shapes=ag_sems(nz),
        compiler_params=pltpu.CompilerParams(
            collective_id=cid, has_side_effects=True, vmem_limit_bytes=48 << 20
        ),
    )(own)


def rs_scratch(nz, c):
    cut = Cuts(c)
    h = nz // 2
    dma = pltpu.SemaphoreType.DMA
    return [
        pltpu.VMEM((2, h + 1, cut.a, LANE), F32),
        pltpu.VMEM((2, h + 1, NX, cut.b, LANE), F32),
        pltpu.VMEM((2, 2, h + 1, cut.a0, LANE), F32),
        pltpu.VMEM((2, 2, h + 1, cut.a, LANE), F32),
        pltpu.VMEM((2, cut.b0, LANE), F32),
        pltpu.VMEM((2, cut.b, LANE), F32),
        dma((2, h + 1)), dma((2, h + 1)), dma((2, h + 1)), dma((2, h + 1)),
        dma((2, 2, h + 1)), dma((2, 2, h + 1)), dma((2, 2, h + 1)), dma((2, 2, h + 1)),
        dma((2, 2)), dma((2, 2)),
    ]


class Scatter:
    def __init__(self, place, part, scratch):
        self.p, self.part = place, part
        self.cut = Cuts(part.shape[2])
        self.h = place.nz // 2
        (self.lza, self.lzb, self.lxh, self.lxa, self.lxbh, self.lxb,
         self.za_s, self.za_r, self.zb_s, self.zb_r,
         self.xh_s, self.xh_r, self.xa_s, self.xa_r, self.xb_s, self.xb_r) = scratch

    def half_len(self, d):
        return self.cut.a0 if d == 0 else self.cut.a - self.cut.a0

    def bhalf_len(self, d):
        return self.cut.b0 if d == 0 else self.cut.b - self.cut.b0

    def xh(self, d, g, s):
        sign = 1 - 2 * d
        zz = self.p.zat((1 - 2 * g) * s)
        return copy_to(
            self.part.at[zz, self.p.xat(2), self.cut.A[1 + d], :],
            self.lxh.at[d, g, s, pl.ds(0, self.half_len(d)), :],
            self.xh_s.at[d, g, s], self.xh_r.at[d, g, s], self.p.dev(0, sign),
        )

    def xa(self, d, g, s):
        sign = 1 - 2 * d
        zz = self.p.zat((1 - 2 * g) * s)
        return copy_to(
            self.part.at[zz, self.p.xat(sign), self.cut.A[0], :],
            self.lxa.at[d, g, s],
            self.xa_s.at[d, g, s], self.xa_r.at[d, g, s], self.p.dev(0, sign),
        )

    def pass_x(self, g, s):
        zz = self.p.zat((1 - 2 * g) * s)
        for d in (0, 1):
            sign = 1 - 2 * d
            self.xh(d, g, s).wait_recv()
            rows = self.cut.A[1 + d]
            xx = self.p.xat(sign)
            self.part[zz, xx, rows, :] = (
                self.part[zz, xx, rows, :] + self.lxh[d, g, s, pl.ds(0, self.half_len(d)), :]
            )
            self.xa(d, g, s).start()

    def sum_x(self, g, s):
        zz = self.p.zat((1 - 2 * g) * s)
        for d in (0, 1):
            self.xa(d, g, s).wait_recv()
        rows = self.cut.A[0]
        self.part[zz, self.p.x, rows, :] = (
            self.part[zz, self.p.x, rows, :] + self.lxa[0, g, s] + self.lxa[1, g, s]
        )

    def za(self, g, s):
        sign = 1 - 2 * g
        return copy_to(
            self.part.at[self.p.zat(sign * s), self.p.x, self.cut.A[0], :],
            self.lza.at[g, s],
            self.za_s.at[g, s], self.za_r.at[g, s], self.p.dev(sign, 0),
        )

    def za_half(self, g):
        sign = 1 - 2 * g
        n = self.half_len(g)
        return copy_to(
            self.part.at[self.p.zat(self.h), self.p.x, self.cut.A[1 + g], :],
            self.lza.at[g, self.h, pl.ds(0, n), :],
            self.za_s.at[g, self.h], self.za_r.at[g, self.h], self.p.dev(sign, 0),
        )

    def zb(self, g, s):
        sign = 1 - 2 * g
        return copy_to(
            self.part.at[self.p.zat(sign * s), :, self.cut.B[0], :],
            self.lzb.at[g, s],
            self.zb_s.at[g, s], self.zb_r.at[g, s], self.p.dev(sign, 0),
        )

    def zb_half(self, g):
        sign = 1 - 2 * g
        xs = pl.ds(g * (NX // 2), NX // 2)
        return copy_to(
            self.part.at[self.p.zat(self.h), xs, self.cut.B[0], :],
            self.lzb.at[g, self.h, pl.ds(0, NX // 2)],
            self.zb_s.at[g, self.h], self.zb_r.at[g, self.h], self.p.dev(sign, 0),
        )

    def xbh(self, d):
        return copy_to(
            self.part.at[self.p.z, self.p.xat(2), self.cut.B[1 + d], :],
            self.lxbh.at[d, pl.ds(0, self.bhalf_len(d)), :],
            self.xb_s.at[0, d], self.xb_r.at[0, d], self.p.dev(0, 1 - 2 * d),
        )

    def xb(self, d):
        sign = 1 - 2 * d
        return copy_to(
            self.part.at[self.p.z, self.p.xat(sign), self.cut.B[0], :],
            self.lxb.at[d],
            self.xb_s.at[1, d], self.xb_r.at[1, d], self.p.dev(0, sign),
        )

    def begin(self):
        h = self.h
        for g in (0, 1):
            self.zb_half(g).start()
        for d in (0, 1):
            self.xh(d, 0, h).start()
        for g in (0, 1):
            for d in (0, 1):
                self.xh(d, g, h - 1).start()
        self.pass_x(0, h)
        for g in (0, 1):
            for d in (0, 1):
                self.xh(d, g, h - 2).start()
        for g in (0, 1):
            self.pass_x(g, h - 1)
        self.sum_x(0, h)
        for g in (0, 1):
            self.za_half(g).start()

    def top(self):
        h = self.h
        s = h - 1
        for g in (0, 1):
            self.zb_half(g).wait_recv()
            zz = self.p.zat((1 - 2 * g) * s)
            xs = pl.ds(g * (NX // 2), NX // 2)
            rows = self.cut.B[0]
            self.part[zz, xs, rows, :] = self.part[zz, xs, rows, :] + self.lzb[g, h, pl.ds(0, NX // 2)]
            self.zb(g, s).start()
        for g in (0, 1):
            for d in (0, 1):
                self.xh(d, g, s - 2).start()
        for g in (0, 1):
            self.pass_x(g, s - 1)
        for g in (0, 1):
            self.sum_x(g, s)
            self.za_half(g).wait_recv()
            zz = self.p.zat((1 - 2 * g) * s)
            rows = self.cut.A[1 + g]
            x = self.p.x
            self.part[zz, x, rows, :] = (
                self.part[zz, x, rows, :] + self.lza[g, h, pl.ds(0, self.half_len(g)), :]
            )
            self.za(g, s).start()

    def ring_b(self, s):
        rows = self.cut.B[0]
        for g in (0, 1):
            self.zb(g, s + 1).wait_recv()
            zz = self.p.zat((1 - 2 * g) * s)
            self.part[zz, :, rows, :] = self.part[zz, :, rows, :] + self.lzb[g, s + 1]
            self.zb(g, s).start()

    def ring_a(self, s):
        rows = self.cut.A[0]
        for g in (0, 1):
            self.sum_x(g, s)
            self.za(g, s + 1).wait_recv()
            zz = self.p.zat((1 - 2 * g) * s)
            self.part[zz, self.p.x, rows, :] = self.part[zz, self.p.x, rows, :] + self.lza[g, s + 1]
            self.za(g, s).start()

    def step(self, s):
        self.ring_b(s)
        if isinstance(s, int) and s <= 2:
            if s == 2:
                for d in (0, 1):
                    self.xh(d, 0, 0).start()
            for g in (0, 1) if s == 2 else (0,):
                self.pass_x(g, s - 1)
        else:
            for g in (0, 1):
                for d in (0, 1):
                    self.xh(d, g, s - 2).start()
            for g in (0, 1):
                self.pass_x(g, s - 1)
        self.ring_a(s)

    def finish(self, out):
        h, cut, p = self.h, self.cut, self.p
        rows = cut.B[0]
        for g in (0, 1):
            self.zb(g, 1).wait_recv()
        self.part[p.z, :, rows, :] = self.part[p.z, :, rows, :] + self.lzb[0, 1] + self.lzb[1, 1]
        for d in (0, 1):
            self.xbh(d).start()
        for d in (0, 1):
            sign = 1 - 2 * d
            self.xbh(d).wait_recv()
            half = cut.B[1 + d]
            xx = p.xat(sign)
            self.part[p.z, xx, half, :] = (
                self.part[p.z, xx, half, :] + self.lxbh[d, pl.ds(0, self.bhalf_len(d)), :]
            )
            self.xb(d).start()
        self.sum_x(0, 0)
        for g in (0, 1):
            self.za(g, 1).wait_recv()
        out[cut.A[0], :] = self.part[p.z, p.x, cut.A[0], :] + self.lza[0, 1] + self.lza[1, 1]
        for d in (0, 1):
            self.xb(d).wait_recv()
        out[rows, :] = self.part[p.z, p.x, rows, :] + self.lxb[0] + self.lxb[1]
        for d in (0, 1):
            self.xh(d, 0, 0).wait_send()
            self.xa(d, 0, 0).wait_send()
            self.xh(d, 0, h).wait_send()
            self.xa(d, 0, h).wait_send()
            self.xb(d).wait_send()
            self.xbh(d).wait_send()
            self.za_half(d).wait_send()
            self.zb_half(d).wait_send()

        def drain(i, _):
            for d in (0, 1):
                self.za(d, i).wait_send()
                self.zb(d, i).wait_send()
                for g in (0, 1):
                    self.xa(d, g, i).wait_send()
                    self.xh(d, g, i).wait_send()
            return _

        lax.fori_loop(1, h, drain, 0)

    def run(self, out):
        self.begin()
        self.top()

        def body(i, _):
            self.step(self.h - 2 - i)
            return _

        lax.fori_loop(0, self.h - 4, body, 0)
        self.step(2)
        self.step(1)
        self.finish(out)


def w_rows(b_ref, l_ref, flat, cols):
    lh, ll = split2(l_ref[...])
    for j in range(0, cols, 256):
        w = dot3(b_ref[:, j : j + 256], (lh, ll), TN)
        for c in range(NX):
            flat[pl.ds(j * NX + c, 256, stride=NX), :] = w[:, c * LANE : (c + 1) * LANE]


def to_chunks(flat, part, c):
    def body(i, _):
        part[i // NX, lax.rem(i, NX)] = flat[pl.ds(pl.multiple_of(i * c, 8), c), :]
        return _

    lax.fori_loop(0, part.shape[0] * NX, body, 0)


def rs_kernel(nz, m_ref, g_ref, l_ref, out_ref, blend, flat, part, *scratch):
    place = Place(nz)
    cols = m_ref.shape[1]
    blend[...] = m_ref[...] + g_ref[...].astype(F32)
    w_rows(blend, l_ref, flat, cols)
    to_chunks(flat, part, out_ref.shape[0])
    greet(place.ring())
    Scatter(place, part, scratch).run(out_ref)


def reduce_scatter(momentum, gradient, left, nz, cid):
    rows, cols = momentum.shape
    c = cols * RANK // LANE // (nz * NX)
    return pl.pallas_call(
        functools.partial(rs_kernel, nz),
        out_shape=jax.ShapeDtypeStruct((c, LANE), F32),
        in_specs=[VMEM] * 3,
        out_specs=VMEM,
        scratch_shapes=[
            pltpu.VMEM((rows, cols), F32),
            pltpu.VMEM((cols * RANK // LANE, LANE), F32),
            pltpu.VMEM((nz, NX, c, LANE), F32),
        ] + rs_scratch(nz, c),
        compiler_params=pltpu.CompilerParams(
            collective_id=cid, has_side_effects=True, vmem_limit_bytes=48 << 20
        ),
    )(momentum, gradient, left)


def left_kernel(nt, m_ref, g_ref, q_ref, out_ref, part, land, s1, r1, s2, r2):
    t = lax.axis_index("tp")
    rows, cols = m_ref.shape
    n = rows // nt
    acc = None
    for j in range(0, cols, 256):
        b = split2(m_ref[:, j : j + 256] + g_ref[:, j : j + 256].astype(F32))
        q = jnp.concatenate(
            [q_ref[pl.ds(j * NX + c, 256, stride=NX), :] for c in range(RANK // LANE)], axis=1
        )
        d = dot3(b, q, NN)
        acc = d if acc is None else acc + d
    part[...] = acc

    def peer(o):
        return lax.rem(t + o, nt)

    greet([{"tp": peer(o)} for o in range(1, nt)])

    def piece(i):
        return pl.ds(pl.multiple_of(i * n, n), n)

    def out1(o):
        return copy_to(part.at[piece(peer(o)), :], land.at[o], s1.at[o], r1.at[o], {"tp": peer(o)})

    def out2(o):
        ref = out_ref.at[piece(t), :]
        return copy_to(ref, ref, s2.at[o], r2.at[o], {"tp": peer(o)})

    for o in range(1, nt):
        out1(o).start()
    total = part[piece(t), :]
    for o in range(1, nt):
        out1(o).wait_recv()
        total = total + land[o]
    out_ref[piece(t), :] = total
    for o in range(1, nt):
        out2(o).start()
    for o in range(1, nt):
        out2(o).wait()
        out1(o).wait_send()


def left_sum(momentum, gradient, q, nt, cid):
    rows = momentum.shape[0]
    dma = pltpu.SemaphoreType.DMA
    return pl.pallas_call(
        functools.partial(left_kernel, nt),
        out_shape=jax.ShapeDtypeStruct((rows, RANK), F32),
        in_specs=[VMEM] * 3,
        out_specs=VMEM,
        scratch_shapes=[
            pltpu.VMEM((rows, RANK), F32),
            pltpu.VMEM((nt, rows // nt, RANK), F32),
            dma((nt,)), dma((nt,)), dma((nt,)), dma((nt,)),
        ],
        compiler_params=pltpu.CompilerParams(
            collective_id=cid, has_side_effects=True, vmem_limit_bytes=48 << 20
        ),
    )(momentum, gradient, q)


def gram_scratch(nz, nt):
    n = RANK // nt // NX
    dma = pltpu.SemaphoreType.DMA
    np_ = n * NX // 8
    return [
        pltpu.VMEM((RANK // nt, RANK), F32),
        pltpu.VMEM((NX, n, RANK), F32),
        pltpu.VMEM((n * NX, LANE), F32),
        pltpu.VMEM((nz, 8, LANE), F32),
        dma((NX,)), dma((NX,)),
        dma((nz,)), dma((nz,)),
        dma((np_,)), dma((np_,)),
        dma((NX,)), dma((NX,)),
        dma((nt,)), dma((nt,)),
    ]


def gram_kernel(nz, nt, l_ref, out_ref, part, landx, flat, landz,
                s1, r1, s2, r2, s3, r3, s4, r4, s5, r5):
    p = Place(nz)
    t = lax.axis_index("tp")
    n = RANK // nt // NX
    pieces = n * NX // 8
    lo = -(pieces // 2)
    offs = [o for o in range(lo, lo + pieces) if o != 0]
    wide = RANK // nt
    left = l_ref[...]
    at = pl.multiple_of(lax.rem(t, LANE // wide) * wide, wide) if wide < LANE else 0
    col = pl.multiple_of(t * wide // LANE * LANE, LANE)
    del at
    tile = l_ref[:, pl.ds(col, LANE)]
    full = dot3(tile, left, TN)
    half = lax.rem(t, LANE // wide)
    mine = full[0:wide]
    for i in range(1, LANE // wide):
        mine = jnp.where(half == i, full[i * wide : (i + 1) * wide], mine)
    part[...] = mine

    greet(
        [p.dev(0, d) for d in range(1, NX)]
        + [p.dev(d, 0) for d in range(1, nz)]
        + [{"tp": lax.rem(t + o, nt)} for o in range(1, nt)]
    )

    def c1(d):
        xx = p.xat(d)
        return copy_to(part.at[pl.ds(pl.multiple_of(xx * n, n), n), :], landx.at[d],
                       s1.at[d], r1.at[d], p.dev(0, d))

    for d in range(1, NX):
        c1(d).start()
    total = part[pl.ds(pl.multiple_of(p.x * n, n), n), :]
    for d in range(1, NX):
        c1(d).wait_recv()
        total = total + landx[d]
    for c in range(RANK // LANE):
        flat[pl.ds(c, n, stride=RANK // LANE), :] = total[:, c * LANE : (c + 1) * LANE]

    def c2(d):
        piece = lax.rem(p.zat(d), pieces)
        return copy_to(flat.at[pl.ds(pl.multiple_of(piece * 8, 8), 8), :], landz.at[p.z],
                       s2.at[d], r2.at[d], p.dev(d, 0))

    for d in range(1, nz):
        c2(d).start()
    own = lax.rem(p.z, pieces)
    landz[p.z] = flat[pl.ds(pl.multiple_of(own * 8, 8), 8), :]
    for d in range(1, nz):
        c2(d).wait_recv()
    tot = landz[0]
    for i in range(1, nz):
        tot = tot + landz[i]
    me = out_ref.at[t, p.x]
    rows = pl.ds(pl.multiple_of(own * 8, 8), 8)
    out_ref[t, p.x, rows, :] = tot

    def c3(i):
        ref = me.at[rows, :]
        return copy_to(ref, ref, s3.at[i], r3.at[i], p.dev(offs[i], 0))

    for i in range(len(offs)):
        c3(i).start()
    for i in range(len(offs)):
        c3(i).wait_recv()

    def c4(d):
        return copy_to(me, me, s4.at[d], r4.at[d], p.dev(0, d))

    for d in range(1, NX):
        c4(d).start()
    for d in range(1, NX):
        c4(d).wait_recv()

    def c5(o):
        ref = out_ref.at[t]
        return copy_to(ref, ref, s5.at[o], r5.at[o], {"tp": lax.rem(t + o, nt)})

    for o in range(1, nt):
        c5(o).start()
    for o in range(1, nt):
        c5(o).wait()
    for d in range(1, NX):
        c4(d).wait_send()
        c1(d).wait_send()
    for i in range(len(offs)):
        c3(i).wait_send()
    for d in range(1, nz):
        c2(d).wait_send()


def gram_sum(left, nz, nt, cid):
    n = RANK // nt // NX
    return pl.pallas_call(
        functools.partial(gram_kernel, nz, nt),
        out_shape=jax.ShapeDtypeStruct((nt, NX, n * RANK // LANE, LANE), F32),
        in_specs=[VMEM],
        out_specs=VMEM,
        scratch_shapes=gram_scratch(nz, nt),
        compiler_params=pltpu.CompilerParams(
            collective_id=cid, has_side_effects=True, vmem_limit_bytes=48 << 20
        ),
    )(left)


BLOCK = 16


def split3(v):
    h = v.astype(BF16)
    r = v - h.astype(F32)
    m = r.astype(BF16)
    return h, m, (r - m.astype(F32)).astype(BF16)


def eliminate(a, at):
    n = a.shape[0]
    wide = a.shape[1] // LANE
    tiles = [a[:, i * LANE : (i + 1) * LANE] for i in range(wide)]
    d = [jnp.broadcast_to(a[:, at + k : at + k + 1], (n, LANE)) for k in range(n)]
    row = lax.broadcasted_iota(jnp.int32, (n, LANE), 0)
    scale = jnp.zeros((n, LANE), F32)
    for k in range(n):
        pivot = d[k][k : k + 1, :]
        r = lax.rsqrt(pivot)
        r = r * (1.5 - 0.5 * pivot * r * r)
        scale = jnp.where(row == k, r, scale)
        if k + 1 < n:
            f = jnp.where(row > k, d[k] * (r * r), 0.0)
            for m in range(k + 1, n):
                d[m] = d[m] - f * d[m][k : k + 1, :]
            tiles = [v - f * v[k : k + 1, :] for v in tiles]
    return jnp.concatenate([v * scale for v in tiles], axis=1)


def chol_panel(zz, p):
    wide = RANK + LANE
    c0 = pl.multiple_of(p * LANE, LANE)
    win = zz.at[pl.ds(c0, LANE), pl.ds(c0, wide)]
    for s in range(0, LANE, BLOCK):
        u = eliminate(win[s : s + BLOCK, :], s)
        win[s : s + BLOCK, :] = u
        if s + BLOCK < LANE:
            h, m, l = split3(u)
            lhs = jnp.concatenate([v[:, :LANE] for v in (h, h, m, h, l, m)], axis=0)
            rhs = jnp.concatenate([h, m, h, l, h, m], axis=0)
            upd = lax.dot_general(lhs, rhs, TN, preferred_element_type=F32)
            win[s + BLOCK :, :] = win[s + BLOCK :, :] - upd[s + BLOCK :, :]

    def below(i, _):
        at = pl.ds(pl.multiple_of(i * LANE, LANE), LANE)
        lhs = zz[pl.ds(c0, LANE), at]
        rest = pl.ds(pl.multiple_of(c0 + LANE, LANE), RANK)
        upd = lax.dot_general(lhs, zz[pl.ds(c0, LANE), rest], TN,
                              precision=lax.Precision.HIGHEST, preferred_element_type=F32)
        zz[at, rest] = zz[at, rest] - upd
        return _

    lax.fori_loop(p + 1, RANK // LANE, below, 0)


def chol_init(zz, g_ref):
    for c in range(RANK // LANE):
        zz[:, c * LANE : (c + 1) * LANE] = g_ref[pl.ds(c, RANK, stride=RANK // LANE), :]
    i = lax.broadcasted_iota(jnp.int32, (RANK, RANK), 0)
    j = lax.broadcasted_iota(jnp.int32, (RANK, RANK), 1)
    zz[:, RANK:] = jnp.where(i == j, 1.0, 0.0).astype(F32)


def chol_kernel(g_ref, out_ref, zz):
    chol_init(zz, g_ref)

    def body(p, _):
        chol_panel(zz, p)
        return _

    lax.fori_loop(0, RANK // LANE, body, 0)
    out_ref[...] = zz[:, RANK:]


def inverse_factor(gram):
    return pl.pallas_call(
        chol_kernel,
        out_shape=jax.ShapeDtypeStruct((RANK, RANK), F32),
        in_specs=[VMEM],
        out_specs=VMEM,
        scratch_shapes=[pltpu.VMEM((RANK, 2 * RANK), F32)],
        compiler_params=pltpu.CompilerParams(vmem_limit_bytes=48 << 20),
    )(gram)


def last_kernel(nt, factor, m_ref, g_ref, l_ref, x_ref, own_ref, w_ref,
                nm_ref, nb_ref, up_ref, wh, wl, sq, land, ss, rs):
    t = lax.axis_index("tp")
    rows, cols = m_ref.shape
    x = split2(x_ref[...])
    total = jnp.zeros((8, RANK), F32)
    for j in range(0, cols, 256):
        w = jnp.concatenate(
            [w_ref[pl.ds(j * NX + c, 256, stride=NX), :] for c in range(RANK // LANE)], axis=1
        )
        h, l = split2(w)
        wh[j : j + 256, :] = h
        wl[j : j + 256, :] = l
        r = dot3((h, l), x, NT)
        total = total + jnp.sum((r * r).reshape(32, 8, RANK), axis=0)
    sq[...] = total

    def peer(o):
        return {"tp": lax.rem(t + o, nt)}

    greet([peer(o) for o in range(1, nt)])

    def send(o):
        return copy_to(sq, land.at[o], ss.at[o], rs.at[o], peer(o))

    for o in range(1, nt):
        send(o).start()
    ortho = dot3(l_ref[...], x, NT)
    m1 = dot3(ortho, x, NN)
    n_own = own_ref.shape[0] // NX
    own = jnp.concatenate(
        [own_ref[pl.ds(c, n_own, stride=NX), :] for c in range(RANK // LANE)], axis=1
    )
    right = dot3(own, x, NT)
    for o in range(1, nt):
        send(o).wait()
        total = total + land[o]
    inv = 1.0 / (jnp.sqrt(jnp.sum(total, axis=0, keepdims=True)) + 1e-06)
    nb_ref[...] = right * inv
    m2 = split2(dot3(ortho * (inv * factor), x, NN))
    m1 = split2(m1 * 0.1)
    for j in range(0, cols, 256):
        w = (wh[j : j + 256, :], wl[j : j + 256, :])
        nm_ref[:, j : j + 256] = (
            m_ref[:, j : j + 256] + g_ref[:, j : j + 256].astype(F32) - dot3(m1, w, NT)
        )
        up_ref[:, j : j + 256] = dot3(m2, w, NT).astype(BF16)


def outputs(momentum, gradient, left, x, own, w, nt, factor, cid):
    rows, cols = momentum.shape
    dma = pltpu.SemaphoreType.DMA
    return pl.pallas_call(
        functools.partial(last_kernel, nt, factor),
        out_shape=(
            jax.ShapeDtypeStruct((rows, cols), F32),
            jax.ShapeDtypeStruct((own.shape[0] // NX, RANK), F32),
            jax.ShapeDtypeStruct((rows, cols), BF16),
        ),
        in_specs=[VMEM] * 6,
        out_specs=(VMEM,) * 3,
        scratch_shapes=[
            pltpu.VMEM((cols, RANK), BF16),
            pltpu.VMEM((cols, RANK), BF16),
            pltpu.VMEM((8, RANK), F32),
            pltpu.VMEM((nt, 8, RANK), F32),
            dma((nt,)), dma((nt,)),
        ],
        compiler_params=pltpu.CompilerParams(
            collective_id=cid, has_side_effects=True, vmem_limit_bytes=48 << 20
        ),
    )(momentum, gradient, left, x, own, w)


def shards(nz, nt, factor, momentum, gradient, right_basis):
    cols = momentum.shape[1]
    q = all_gather(right_basis.reshape(-1, LANE), nz, 1)
    left = left_sum(momentum, gradient, q.reshape(-1, LANE), nt, 2)
    gram = gram_sum(left, nz, nt, 3)
    own = reduce_scatter(momentum, gradient, left, nz, 4)
    w = all_gather(own, nz, 5)
    x = inverse_factor(gram.reshape(-1, LANE))
    return outputs(momentum, gradient, left, x, own, w.reshape(-1, LANE), nt, factor, 6)


def solution(mesh):
    nz = mesh.shape["fsdp"] // NX
    nt = mesh.shape["tp"]
    factor = (float(ROWS) * COLS / RANK) ** 0.5
    placed = (P("fsdp", "tp"), P("fsdp", "tp"), P(("tp", "fsdp"), None))
    return jax.shard_map(
        functools.partial(shards, nz, nt, factor),
        mesh=mesh,
        in_specs=placed,
        out_specs=(P("fsdp", "tp"), P(("tp", "fsdp"), None), P("fsdp", "tp")),
        check_vma=False,
    )
```

```python
import functools

import jax
import jax.numpy as jnp
from jax import lax
from jax.experimental import pallas as pl
from jax.experimental.pallas import tpu as pltpu
from jax.sharding import PartitionSpec as P

ROWS = 8192
COLS = 14336
RANK = 512
MESH = pl.DeviceIdType.MESH
LANE = 128
NX = 4
VMEM = pl.BlockSpec(memory_space=pltpu.VMEM)
F32 = jnp.float32
BF16 = jnp.bfloat16
NN = (((1,), (0,)), ((), ()))
TN = (((0,), (0,)), ((), ()))
NT = (((1,), (1,)), ((), ()))


def split2(v):
    hi = v.astype(BF16)
    return hi, (v - hi.astype(F32)).astype(BF16)


def dot3(a, b, dims):
    ah, al = a if isinstance(a, tuple) else split2(a)
    bh, bl = b if isinstance(b, tuple) else split2(b)
    d = functools.partial(lax.dot_general, dimension_numbers=dims, preferred_element_type=F32)
    return d(ah, bh) + (d(ah, bl) + d(al, bh))


def copy_to(src, dst, send, recv, where):
    return pltpu.make_async_remote_copy(
        src_ref=src, dst_ref=dst, send_sem=send, recv_sem=recv, device_id=where, device_id_type=MESH
    )


def greet(peers):
    barrier = pltpu.get_barrier_semaphore()
    for peer in peers:
        pl.semaphore_signal(barrier, inc=1, device_id=peer, device_id_type=MESH)
    pl.semaphore_wait(barrier, len(peers))


class Place:
    def __init__(self, nz):
        me = lax.axis_index("fsdp")
        self.nz = nz
        self.z = me // NX
        self.x = lax.rem(me, NX)

    def zat(self, d):
        return lax.rem(self.z + (d + self.nz), self.nz)

    def xat(self, d):
        return lax.rem(self.x + (d + NX), NX)

    def dev(self, dz, dx):
        return {"fsdp": self.zat(dz) * NX + self.xat(dx)}

    def near(self):
        zs = NEAR + (3, -3, HUB, -HUB)
        return [self.dev(d, 0) for d in zs] + [self.dev(0, 1), self.dev(0, -1)]


HUB = 5
NEAR = (1, -1, 2, -2)
FAR = (4, -4, 6, -6, 3, -3, 7, -7, 8)
NOFF = 17


def halves(c):
    return (pl.ds(0, c // 2), pl.ds(c // 2, c // 2))


def ag_sems():
    dma = pltpu.SemaphoreType.DMA
    return [dma((NOFF,)), dma((NOFF,))] + [dma((2, NOFF))] * 4


class Gather:
    order = NEAR + (HUB, -HUB) + FAR

    def __init__(self, place, out, sems):
        self.p, self.out = place, out
        self.half = halves(out.shape[2])
        self.zs, self.zr, self.xs, self.xr, self.hs, self.hr = sems

    def zc(self, o):
        p, i = self.p, o + 8
        if o in NEAR or abs(o) == HUB:
            ref, to = self.out.at[p.z, p.x], o
        else:
            hub = HUB if o > 0 else -HUB
            ref, to = self.out.at[p.zat(-hub), p.x], o - hub
            if abs(o) == 8:
                ref = ref.at[self.half[0 if o > 0 else 1], :]
        return copy_to(ref, ref, self.zs.at[i], self.zr.at[i], p.dev(to, 0))

    def xa(self, d, o):
        ref = self.out.at[self.p.zat(-o), self.p.x]
        return copy_to(ref, ref, self.xs.at[d, o + 8], self.xr.at[d, o + 8], self.p.dev(0, 1 - 2 * d))

    def xh(self, d, o):
        sign = 1 - 2 * d
        ref = self.out.at[self.p.zat(-o), self.p.xat(-sign), self.half[d], :]
        return copy_to(ref, ref, self.hs.at[d, o + 8], self.hr.at[d, o + 8], self.p.dev(0, sign))

    def begin(self):
        for d in (0, 1):
            self.xa(d, 0).start()
        for o in (HUB, -HUB) + NEAR:
            self.zc(o).start()

    def arrive(self, o):
        self.zc(o).wait_recv()
        if abs(o) == HUB:
            for j in NEAR + ((3,) if o > 0 else (-3,)):
                self.zc(o + j).start()
        if o == 8:
            self.zc(-8).wait_recv()
        for d in (0, 1):
            self.xa(d, o).start()

    def onward(self, o):
        for d in (0, 1):
            self.xa(d, o).wait_recv()
            self.xh(d, o).start()

    def events(self):
        lag = 3
        out = []
        groups = (0,) + self.order
        for i in range(1, len(groups) + lag):
            todo = []
            if i < len(groups):
                todo.append(functools.partial(self.arrive, groups[i]))
            if 0 <= i - lag < len(groups):
                todo.append(functools.partial(self.onward, groups[i - lag]))
            out.append(todo)
        return out

    def finish(self):
        for o in (0,) + self.order:
            for d in (0, 1):
                self.xh(d, o).wait()
                self.xa(d, o).wait_send()
            if o:
                self.zc(o).wait_send()
        self.zc(-8).wait_send()


def ag_kernel(nz, own_ref, out_ref, *sems):
    place = Place(nz)
    out_ref[place.z, place.x] = own_ref[...]
    greet(place.near())
    gather = Gather(place, out_ref, sems)
    gather.begin()
    for todo in gather.events():
        for f in todo:
            f()
    gather.finish()


def all_gather(own, nz, cid):
    c = own.shape[0]
    return pl.pallas_call(
        functools.partial(ag_kernel, nz),
        out_shape=jax.ShapeDtypeStruct((nz, NX, c, LANE), F32),
        in_specs=[VMEM],
        out_specs=VMEM,
        scratch_shapes=ag_sems(),
        compiler_params=pltpu.CompilerParams(
            collective_id=cid, has_side_effects=True, vmem_limit_bytes=48 << 20
        ),
    )(own)


def ag_chol_kernel(nz, own_ref, g_ref, out_ref, x_ref, zz, *sems):
    place = Place(nz)
    out_ref[place.z, place.x] = own_ref[...]
    greet(place.near())
    gather = Gather(place, out_ref, sems)
    gather.begin()
    chol_init(zz, g_ref)
    events = gather.events()
    blocks = LANE // BLOCK

    def between(p, s):
        for pp in range(RANK // LANE):
            at = pp * blocks + s
            if at % 2 == 1 and at // 2 < len(events):

                @pl.when(p == pp)
                def _(at=at):
                    for f in events[at // 2]:
                        f()

    def body(p, _):
        chol_panel(zz, p, between)
        return _

    lax.fori_loop(0, RANK // LANE, body, 0)
    for todo in events[RANK // BLOCK // 2 :]:
        for f in todo:
            f()
    x_ref[...] = zz[:, RANK:]
    gather.finish()


def gather_and_factor(own, gram, nz, cid):
    c = own.shape[0]
    return pl.pallas_call(
        functools.partial(ag_chol_kernel, nz),
        out_shape=(
            jax.ShapeDtypeStruct((nz, NX, c, LANE), F32),
            jax.ShapeDtypeStruct((RANK, RANK), F32),
        ),
        in_specs=[VMEM] * 2,
        out_specs=(VMEM,) * 2,
        scratch_shapes=[pltpu.VMEM((RANK, 2 * RANK), F32)] + ag_sems(),
        compiler_params=pltpu.CompilerParams(
            collective_id=cid, has_side_effects=True, vmem_limit_bytes=48 << 20
        ),
    )(own, gram)


def rs_scratch(c):
    dma = pltpu.SemaphoreType.DMA
    return [
        pltpu.VMEM((NOFF, c, LANE), F32),
        pltpu.VMEM((2, NOFF, c // 2, LANE), F32),
        pltpu.VMEM((2, NOFF, c, LANE), F32),
        dma((NOFF,)), dma((NOFF,)),
    ] + [dma((2, NOFF))] * 4


class Scatter:
    order = (8, 3, -3, 4, -4, 6, -6, 7, -7, HUB, -HUB, 1, -1, 2, -2, 0)

    def __init__(self, place, part, scratch):
        self.p, self.part = place, part
        self.half = halves(part.shape[2])
        self.n = part.shape[2]
        self.lz, self.lh, self.la, self.zs, self.zr, self.xs, self.xr, self.hs, self.hr = scratch

    def xh(self, d, o):
        p = self.p
        return copy_to(
            self.part.at[p.zat(o), p.xat(2), self.half[d], :], self.lh.at[d, o + 8],
            self.hs.at[d, o + 8], self.hr.at[d, o + 8], p.dev(0, 1 - 2 * d),
        )

    def xa(self, d, o):
        p, sign = self.p, 1 - 2 * d
        return copy_to(
            self.part.at[p.zat(o), p.xat(sign)], self.la.at[d, o + 8],
            self.xs.at[d, o + 8], self.xr.at[d, o + 8], p.dev(0, sign),
        )

    def zc(self, o):
        p, i = self.p, o + 8
        ref, land, to = self.part.at[p.zat(o), p.x], self.lz.at[i], o
        if o not in NEAR and abs(o) != HUB:
            to = o - (HUB if o > 0 else -HUB)
            if abs(o) == 8:
                rows = self.half[0 if o > 0 else 1]
                ref, land = ref.at[rows, :], land.at[rows, :]
        return copy_to(ref, land, self.zs.at[i], self.zr.at[i], p.dev(to, 0))

    def ahead(self, o):
        for d in (0, 1):
            self.xh(d, o).start()

    def pass_x(self, o):
        p = self.p
        zz = p.zat(o)
        for d in (0, 1):
            self.xh(d, o).wait_recv()
            rows, xx = self.half[d], p.xat(1 - 2 * d)
            self.part[zz, xx, rows, :] = self.part[zz, xx, rows, :] + self.lh[d, o + 8]
            self.xa(d, o).start()

    def sum_x(self, o):
        p = self.p
        zz = p.zat(o)
        for d in (0, 1):
            self.xa(d, o).wait_recv()
        self.part[zz, p.x] = self.part[zz, p.x] + self.la[0, o + 8] + self.la[1, o + 8]
        if o == 8:
            self.zc(8).start()
            self.zc(-8).start()
        elif o and abs(o) != HUB:
            self.zc(o).start()

    def hub(self, o):
        p = self.p
        zz = p.zat(o)
        total = self.part[zz, p.x]
        for j in NEAR:
            self.zc(o + j).wait_recv()
            total = total + self.lz[o + j + 8]
        self.part[zz, p.x] = total
        i = 0 if o > 0 else 1
        end = 8 if o > 0 else -8
        self.zc(end).wait_recv()
        rows = self.half[i]
        self.part[zz, p.x, rows, :] = self.part[zz, p.x, rows, :] + self.lz[end + 8, rows, :]
        self.zc(o).start()

    def run(self, out, others):
        g = self.order
        lag = 3
        for o in g[:lag]:
            self.ahead(o)
        for i in range(len(g) + lag):
            if i + lag < len(g):
                self.ahead(g[i + lag])
            if i < len(g):
                self.pass_x(g[i])
            if i >= lag:
                self.sum_x(g[i - lag])
                if g[i - lag] == 1:
                    self.hub(HUB)
                if g[i - lag] == -1:
                    self.hub(-HUB)
            if i in others:
                others[i]()
        total = self.part[self.p.z, self.p.x]
        for o in NEAR + (HUB, -HUB):
            self.zc(o).wait_recv()
            total = total + self.lz[o + 8]
        out[...] = total
        for o in g:
            for d in (0, 1):
                self.xh(d, o).wait_send()
                self.xa(d, o).wait_send()
            if o:
                self.zc(o).wait_send()
        self.zc(-8).wait_send()


def w_rows(b_ref, l_ref, flat, cols):
    lh, ll = split2(l_ref[...])
    for j in range(0, cols, 256):
        w = dot3(b_ref[:, j : j + 256], (lh, ll), TN)
        for c in range(NX):
            flat[pl.ds(j * NX + c, 256, stride=NX), :] = w[:, c * LANE : (c + 1) * LANE]


def to_chunks(flat, part, c):
    def body(i, _):
        part[i // NX, lax.rem(i, NX)] = flat[pl.ds(pl.multiple_of(i * c, 8), c), :]
        return _

    lax.fori_loop(0, part.shape[0] * NX, body, 0)


def rs_kernel(nz, nt, m_ref, g_ref, l_ref, out_ref, gram_ref, blend, flat, part, *scratch):
    place = Place(nz)
    cols = m_ref.shape[1]
    n_rs = len(rs_scratch(8))
    gram = Gram(place, nt, gram_ref, scratch[n_rs:])
    gram.compute(l_ref)
    zs = [place.dev(d, 0) for d in range(1, nz)]
    xs = [place.dev(0, d) for d in range(1, NX)]
    greet(zs + xs + [gram.peer(o) for o in range(1, nt)])
    gram.stage1()
    blend[...] = m_ref[...] + g_ref[...].astype(F32)
    w_rows(blend, l_ref, flat, cols)
    to_chunks(flat, part, out_ref.shape[0])
    gram.stage2()
    others = {3: gram.stage3, 6: gram.stage4, 9: gram.stage5}
    Scatter(place, part, scratch[:n_rs]).run(out_ref, others)
    gram.finish()


def scatter_and_gram(momentum, gradient, left, nz, nt, cid):
    rows, cols = momentum.shape
    c = cols * RANK // LANE // (nz * NX)
    n = RANK // nt // NX
    return pl.pallas_call(
        functools.partial(rs_kernel, nz, nt),
        out_shape=(
            jax.ShapeDtypeStruct((c, LANE), F32),
            jax.ShapeDtypeStruct((nt, NX, n * RANK // LANE, LANE), F32),
        ),
        in_specs=[VMEM] * 3,
        out_specs=(VMEM,) * 2,
        scratch_shapes=[
            pltpu.VMEM((rows, cols), F32),
            pltpu.VMEM((cols * RANK // LANE, LANE), F32),
            pltpu.VMEM((nz, NX, c, LANE), F32),
        ] + rs_scratch(c) + gram_scratch(nz, nt),
        compiler_params=pltpu.CompilerParams(
            collective_id=cid, has_side_effects=True, vmem_limit_bytes=48 << 20
        ),
    )(momentum, gradient, left)


def left_kernel(nt, m_ref, g_ref, q_ref, out_ref, part, land, s1, r1, s2, r2):
    t = lax.axis_index("tp")
    rows, cols = m_ref.shape
    n = rows // nt
    acc = None
    for j in range(0, cols, 256):
        b = split2(m_ref[:, j : j + 256] + g_ref[:, j : j + 256].astype(F32))
        q = jnp.concatenate(
            [q_ref[pl.ds(j * NX + c, 256, stride=NX), :] for c in range(RANK // LANE)], axis=1
        )
        d = dot3(b, q, NN)
        acc = d if acc is None else acc + d
    part[...] = acc

    def peer(o):
        return lax.rem(t + o, nt)

    greet([{"tp": peer(o)} for o in range(1, nt)])

    def piece(i):
        return pl.ds(pl.multiple_of(i * n, n), n)

    def out1(o):
        return copy_to(part.at[piece(peer(o)), :], land.at[o], s1.at[o], r1.at[o], {"tp": peer(o)})

    def out2(o):
        ref = out_ref.at[piece(t), :]
        return copy_to(ref, ref, s2.at[o], r2.at[o], {"tp": peer(o)})

    for o in range(1, nt):
        out1(o).start()
    total = part[piece(t), :]
    for o in range(1, nt):
        out1(o).wait_recv()
        total = total + land[o]
    out_ref[piece(t), :] = total
    for o in range(1, nt):
        out2(o).start()
    for o in range(1, nt):
        out2(o).wait()
        out1(o).wait_send()


def left_sum(momentum, gradient, q, nt, cid):
    rows = momentum.shape[0]
    dma = pltpu.SemaphoreType.DMA
    return pl.pallas_call(
        functools.partial(left_kernel, nt),
        out_shape=jax.ShapeDtypeStruct((rows, RANK), F32),
        in_specs=[VMEM] * 3,
        out_specs=VMEM,
        scratch_shapes=[
            pltpu.VMEM((rows, RANK), F32),
            pltpu.VMEM((nt, rows // nt, RANK), F32),
            dma((nt,)), dma((nt,)), dma((nt,)), dma((nt,)),
        ],
        compiler_params=pltpu.CompilerParams(
            collective_id=cid, has_side_effects=True, vmem_limit_bytes=48 << 20
        ),
    )(momentum, gradient, q)


def gram_scratch(nz, nt):
    n = RANK // nt // NX
    dma = pltpu.SemaphoreType.DMA
    np_ = n * NX // 8
    return [
        pltpu.VMEM((RANK // nt, RANK), F32),
        pltpu.VMEM((NX, n, RANK), F32),
        pltpu.VMEM((n * NX, LANE), F32),
        pltpu.VMEM((nz, 8, LANE), F32),
        dma((NX,)), dma((NX,)),
        dma((nz,)), dma((nz,)),
        dma((np_,)), dma((np_,)),
        dma((NX,)), dma((NX,)),
        dma((nt,)), dma((nt,)),
    ]


class Gram:
    def __init__(self, place, nt, out, scratch):
        self.p, self.nt, self.out = place, nt, out
        (self.part, self.landx, self.flat, self.landz, self.s1, self.r1, self.s2, self.r2,
         self.s3, self.r3, self.s4, self.r4, self.s5, self.r5) = scratch
        self.t = lax.axis_index("tp")
        self.n = RANK // nt // NX
        self.pieces = self.n * NX // 8
        lo = -(self.pieces // 2)
        self.offs = [o for o in range(lo, lo + self.pieces) if o != 0]
        self.own = lax.rem(place.z, self.pieces)
        self.me = out.at[self.t, place.x]
        self.rows = pl.ds(pl.multiple_of(self.own * 8, 8), 8)

    def peer(self, o):
        return {"tp": lax.rem(self.t + o, self.nt)}

    def compute(self, l_ref):
        wide = RANK // self.nt
        col = pl.multiple_of(self.t * wide // LANE * LANE, LANE)
        full = dot3(l_ref[:, pl.ds(col, LANE)], l_ref[...], TN)
        which = lax.rem(self.t, LANE // wide)
        mine = full[0:wide]
        for i in range(1, LANE // wide):
            mine = jnp.where(which == i, full[i * wide : (i + 1) * wide], mine)
        self.part[...] = mine

    def c1(self, d):
        xx = self.p.xat(d)
        n = self.n
        return copy_to(self.part.at[pl.ds(pl.multiple_of(xx * n, n), n), :], self.landx.at[d],
                       self.s1.at[d], self.r1.at[d], self.p.dev(0, d))

    def c2(self, d):
        piece = lax.rem(self.p.zat(d), self.pieces)
        return copy_to(self.flat.at[pl.ds(pl.multiple_of(piece * 8, 8), 8), :],
                       self.landz.at[self.p.z], self.s2.at[d], self.r2.at[d], self.p.dev(d, 0))

    def c3(self, i):
        ref = self.me.at[self.rows, :]
        return copy_to(ref, ref, self.s3.at[i], self.r3.at[i], self.p.dev(self.offs[i], 0))

    def c4(self, d):
        return copy_to(self.me, self.me, self.s4.at[d], self.r4.at[d], self.p.dev(0, d))

    def c5(self, o):
        ref = self.out.at[self.t]
        return copy_to(ref, ref, self.s5.at[o], self.r5.at[o], self.peer(o))

    def stage1(self):
        for d in range(1, NX):
            self.c1(d).start()

    def stage2(self):
        n = self.n
        total = self.part[pl.ds(pl.multiple_of(self.p.x * n, n), n), :]
        for d in range(1, NX):
            self.c1(d).wait_recv()
            total = total + self.landx[d]
        for c in range(RANK // LANE):
            self.flat[pl.ds(c, n, stride=RANK // LANE), :] = total[:, c * LANE : (c + 1) * LANE]
        for d in range(1, self.p.nz):
            self.c2(d).start()
        self.landz[self.p.z] = self.flat[self.rows, :]

    def stage3(self):
        for d in range(1, self.p.nz):
            self.c2(d).wait_recv()
        tot = self.landz[0]
        for i in range(1, self.p.nz):
            tot = tot + self.landz[i]
        self.out[self.t, self.p.x, self.rows, :] = tot
        for i in range(len(self.offs)):
            self.c3(i).start()

    def stage4(self):
        for i in range(len(self.offs)):
            self.c3(i).wait_recv()
        for d in range(1, NX):
            self.c4(d).start()

    def stage5(self):
        for d in range(1, NX):
            self.c4(d).wait_recv()
        for o in range(1, self.nt):
            self.c5(o).start()

    def finish(self):
        for o in range(1, self.nt):
            self.c5(o).wait()
        for d in range(1, NX):
            self.c4(d).wait_send()
            self.c1(d).wait_send()
        for i in range(len(self.offs)):
            self.c3(i).wait_send()
        for d in range(1, self.p.nz):
            self.c2(d).wait_send()


BLOCK = 16


def split3(v):
    h = v.astype(BF16)
    r = v - h.astype(F32)
    m = r.astype(BF16)
    return h, m, (r - m.astype(F32)).astype(BF16)


def eliminate(a, at):
    n = a.shape[0]
    wide = a.shape[1] // LANE
    tiles = [a[:, i * LANE : (i + 1) * LANE] for i in range(wide)]
    d = [jnp.broadcast_to(a[:, at + k : at + k + 1], (n, LANE)) for k in range(n)]
    row = lax.broadcasted_iota(jnp.int32, (n, LANE), 0)
    scale = jnp.zeros((n, LANE), F32)
    for k in range(n):
        pivot = d[k][k : k + 1, :]
        r = lax.rsqrt(pivot)
        r = r * (1.5 - 0.5 * pivot * r * r)
        scale = jnp.where(row == k, r, scale)
        if k + 1 < n:
            f = jnp.where(row > k, d[k] * (r * r), 0.0)
            for m in range(k + 1, n):
                d[m] = d[m] - f * d[m][k : k + 1, :]
            tiles = [v - f * v[k : k + 1, :] for v in tiles]
    return jnp.concatenate([v * scale for v in tiles], axis=1)


def chol_panel(zz, p, between):
    wide = RANK + LANE
    c0 = pl.multiple_of(p * LANE, LANE)
    win = zz.at[pl.ds(c0, LANE), pl.ds(c0, wide)]
    for s in range(0, LANE, BLOCK):
        u = eliminate(win[s : s + BLOCK, :], s)
        win[s : s + BLOCK, :] = u
        if s + BLOCK < LANE:
            h, m, l = split3(u)
            lhs = jnp.concatenate([v[:, :LANE] for v in (h, h, m, h, l, m)], axis=0)
            rhs = jnp.concatenate([h, m, h, l, h, m], axis=0)
            upd = lax.dot_general(lhs, rhs, TN, preferred_element_type=F32)
            win[s + BLOCK :, :] = win[s + BLOCK :, :] - upd[s + BLOCK :, :]
        between(p, s // BLOCK)

    def below(i, _):
        at = pl.ds(pl.multiple_of(i * LANE, LANE), LANE)
        lhs = zz[pl.ds(c0, LANE), at]
        rest = pl.ds(pl.multiple_of(c0 + LANE, LANE), RANK)
        upd = lax.dot_general(lhs, zz[pl.ds(c0, LANE), rest], TN,
                              precision=lax.Precision.HIGHEST, preferred_element_type=F32)
        zz[at, rest] = zz[at, rest] - upd
        return _

    lax.fori_loop(p + 1, RANK // LANE, below, 0)


def chol_init(zz, g_ref):
    for c in range(RANK // LANE):
        zz[:, c * LANE : (c + 1) * LANE] = g_ref[pl.ds(c, RANK, stride=RANK // LANE), :]
    i = lax.broadcasted_iota(jnp.int32, (RANK, RANK), 0)
    j = lax.broadcasted_iota(jnp.int32, (RANK, RANK), 1)
    zz[:, RANK:] = jnp.where(i == j, 1.0, 0.0).astype(F32)


def last_kernel(nt, factor, m_ref, g_ref, l_ref, x_ref, own_ref, w_ref,
                nm_ref, nb_ref, up_ref, wh, wl, sq, land, ss, rs):
    t = lax.axis_index("tp")
    rows, cols = m_ref.shape
    x = split2(x_ref[...])
    total = jnp.zeros((8, RANK), F32)
    for j in range(0, cols, 256):
        w = jnp.concatenate(
            [w_ref[pl.ds(j * NX + c, 256, stride=NX), :] for c in range(RANK // LANE)], axis=1
        )
        h, l = split2(w)
        wh[j : j + 256, :] = h
        wl[j : j + 256, :] = l
        r = dot3((h, l), x, NT)
        total = total + jnp.sum((r * r).reshape(32, 8, RANK), axis=0)
    sq[...] = total

    def peer(o):
        return {"tp": lax.rem(t + o, nt)}

    greet([peer(o) for o in range(1, nt)])

    def send(o):
        return copy_to(sq, land.at[o], ss.at[o], rs.at[o], peer(o))

    for o in range(1, nt):
        send(o).start()
    ortho = dot3(l_ref[...], x, NT)
    m1 = dot3(ortho, x, NN)
    n_own = own_ref.shape[0] // NX
    own = jnp.concatenate(
        [own_ref[pl.ds(c, n_own, stride=NX), :] for c in range(RANK // LANE)], axis=1
    )
    right = dot3(own, x, NT)
    for o in range(1, nt):
        send(o).wait()
        total = total + land[o]
    inv = 1.0 / (jnp.sqrt(jnp.sum(total, axis=0, keepdims=True)) + 1e-06)
    nb_ref[...] = right * inv
    m2 = split2(dot3(ortho * (inv * factor), x, NN))
    m1 = split2(m1 * 0.1)
    for j in range(0, cols, 256):
        w = (wh[j : j + 256, :], wl[j : j + 256, :])
        nm_ref[:, j : j + 256] = (
            m_ref[:, j : j + 256] + g_ref[:, j : j + 256].astype(F32) - dot3(m1, w, NT)
        )
        up_ref[:, j : j + 256] = dot3(m2, w, NT).astype(BF16)


def outputs(momentum, gradient, left, x, own, w, nt, factor, cid):
    rows, cols = momentum.shape
    dma = pltpu.SemaphoreType.DMA
    return pl.pallas_call(
        functools.partial(last_kernel, nt, factor),
        out_shape=(
            jax.ShapeDtypeStruct((rows, cols), F32),
            jax.ShapeDtypeStruct((own.shape[0] // NX, RANK), F32),
            jax.ShapeDtypeStruct((rows, cols), BF16),
        ),
        in_specs=[VMEM] * 6,
        out_specs=(VMEM,) * 3,
        scratch_shapes=[
            pltpu.VMEM((cols, RANK), BF16),
            pltpu.VMEM((cols, RANK), BF16),
            pltpu.VMEM((8, RANK), F32),
            pltpu.VMEM((nt, 8, RANK), F32),
            dma((nt,)), dma((nt,)),
        ],
        compiler_params=pltpu.CompilerParams(
            collective_id=cid, has_side_effects=True, vmem_limit_bytes=48 << 20
        ),
    )(momentum, gradient, left, x, own, w)


def shards(nz, nt, factor, momentum, gradient, right_basis):
    cols = momentum.shape[1]
    q = all_gather(right_basis.reshape(-1, LANE), nz, 1)
    left = left_sum(momentum, gradient, q.reshape(-1, LANE), nt, 2)
    own, gram = scatter_and_gram(momentum, gradient, left, nz, nt, 3)
    w, x = gather_and_factor(own, gram.reshape(-1, LANE), nz, 4)
    return outputs(momentum, gradient, left, x, own, w.reshape(-1, LANE), nt, factor, 5)


def solution(mesh):
    nz = mesh.shape["fsdp"] // NX
    nt = mesh.shape["tp"]
    factor = (float(ROWS) * COLS / RANK) ** 0.5
    placed = (P("fsdp", "tp"), P("fsdp", "tp"), P(("tp", "fsdp"), None))
    return jax.shard_map(
        functools.partial(shards, nz, nt, factor),
        mesh=mesh,
        in_specs=placed,
        out_specs=(P("fsdp", "tp"), P(("tp", "fsdp"), None), P("fsdp", "tp")),
        check_vma=False,
    )
```

```python
import functools

import jax
import jax.numpy as jnp
from jax import lax
from jax.experimental import pallas as pl
from jax.experimental.pallas import tpu as pltpu
from jax.sharding import PartitionSpec as P

ROWS = 8192
COLS = 14336
RANK = 512
MESH = pl.DeviceIdType.MESH
LANE = 128
NX = 4
VMEM = pl.BlockSpec(memory_space=pltpu.VMEM)
F32 = jnp.float32
BF16 = jnp.bfloat16
NN = (((1,), (0,)), ((), ()))
TN = (((0,), (0,)), ((), ()))
NT = (((1,), (1,)), ((), ()))


def split2(v):
    hi = v.astype(BF16)
    return hi, (v - hi.astype(F32)).astype(BF16)


def dot3(a, b, dims):
    ah, al = a if isinstance(a, tuple) else split2(a)
    bh, bl = b if isinstance(b, tuple) else split2(b)
    d = functools.partial(lax.dot_general, dimension_numbers=dims, preferred_element_type=F32)
    return d(ah, bh) + (d(ah, bl) + d(al, bh))


def copy_to(src, dst, send, recv, where):
    return pltpu.make_async_remote_copy(
        src_ref=src, dst_ref=dst, send_sem=send, recv_sem=recv, device_id=where, device_id_type=MESH
    )


def greet(peers):
    barrier = pltpu.get_barrier_semaphore()
    for peer in peers:
        pl.semaphore_signal(barrier, inc=1, device_id=peer, device_id_type=MESH)
    pl.semaphore_wait(barrier, len(peers))


class Place:
    def __init__(self, nz):
        me = lax.axis_index("fsdp")
        self.nz = nz
        self.z = me // NX
        self.x = lax.rem(me, NX)

    def zat(self, d):
        return lax.rem(self.z + (d + self.nz), self.nz)

    def xat(self, d):
        return lax.rem(self.x + (d + NX), NX)

    def dev(self, dz, dx):
        return {"fsdp": self.zat(dz) * NX + self.xat(dx)}

    def near(self):
        zs = NEAR + (3, -3, HUB, -HUB)
        return [self.dev(d, 0) for d in zs] + [self.dev(0, 1), self.dev(0, -1)]


HUB = 5
NEAR = (1, -1, 2, -2)
FAR = (4, -4, 6, -6, 3, -3, 7, -7, 8)
NOFF = 17


def halves(c):
    return (pl.ds(0, c // 2), pl.ds(c // 2, c // 2))


def ag_sems():
    dma = pltpu.SemaphoreType.DMA
    return [dma((NOFF,)), dma((NOFF,))] + [dma((2, NOFF))] * 4


class Gather:
    order = NEAR + (HUB, -HUB) + FAR

    def __init__(self, place, out, sems):
        self.p, self.out = place, out
        self.half = halves(out.shape[2])
        self.zs, self.zr, self.xs, self.xr, self.hs, self.hr = sems

    def zc(self, o):
        p, i = self.p, o + 8
        if o in NEAR or abs(o) == HUB:
            ref, to = self.out.at[p.z, p.x], o
        else:
            hub = HUB if o > 0 else -HUB
            ref, to = self.out.at[p.zat(-hub), p.x], o - hub
            if abs(o) == 8:
                ref = ref.at[self.half[0 if o > 0 else 1], :]
        return copy_to(ref, ref, self.zs.at[i], self.zr.at[i], p.dev(to, 0))

    def xa(self, d, o):
        ref = self.out.at[self.p.zat(-o), self.p.x]
        return copy_to(ref, ref, self.xs.at[d, o + 8], self.xr.at[d, o + 8], self.p.dev(0, 1 - 2 * d))

    def xh(self, d, o):
        sign = 1 - 2 * d
        ref = self.out.at[self.p.zat(-o), self.p.xat(-sign), self.half[d], :]
        return copy_to(ref, ref, self.hs.at[d, o + 8], self.hr.at[d, o + 8], self.p.dev(0, sign))

    def begin(self):
        for d in (0, 1):
            self.xa(d, 0).start()
        for o in (HUB, -HUB) + NEAR:
            self.zc(o).start()

    def arrive(self, o):
        self.zc(o).wait_recv()
        if abs(o) == HUB:
            for j in NEAR + ((3,) if o > 0 else (-3,)):
                self.zc(o + j).start()
        if o == 8:
            self.zc(-8).wait_recv()
        for d in (0, 1):
            self.xa(d, o).start()

    def onward(self, o):
        for d in (0, 1):
            self.xa(d, o).wait_recv()
            self.xh(d, o).start()

    def events(self):
        lag = 3
        out = []
        groups = (0,) + self.order
        for i in range(1, len(groups) + lag):
            todo = []
            if i < len(groups):
                todo.append(functools.partial(self.arrive, groups[i]))
            if 0 <= i - lag < len(groups):
                todo.append(functools.partial(self.onward, groups[i - lag]))
            out.append(todo)
        return out

    def finish(self):
        for o in (0,) + self.order:
            for d in (0, 1):
                self.xh(d, o).wait()
                self.xa(d, o).wait_send()
            if o:
                self.zc(o).wait_send()
        self.zc(-8).wait_send()


def rs_scratch(c):
    dma = pltpu.SemaphoreType.DMA
    return [
        pltpu.VMEM((NOFF, c, LANE), F32),
        pltpu.VMEM((2, NOFF, c // 2, LANE), F32),
        pltpu.VMEM((2, NOFF, c, LANE), F32),
        dma((NOFF,)), dma((NOFF,)),
    ] + [dma((2, NOFF))] * 4


class Scatter:
    order = (8, 3, -3, 4, -4, 6, -6, 7, -7, HUB, -HUB, 1, -1, 2, -2, 0)

    def __init__(self, place, part, scratch):
        self.p, self.part = place, part
        self.half = halves(part.shape[2])
        self.n = part.shape[2]
        self.lz, self.lh, self.la, self.zs, self.zr, self.xs, self.xr, self.hs, self.hr = scratch

    def xh(self, d, o):
        p = self.p
        return copy_to(
            self.part.at[p.zat(o), p.xat(2), self.half[d], :], self.lh.at[d, o + 8],
            self.hs.at[d, o + 8], self.hr.at[d, o + 8], p.dev(0, 1 - 2 * d),
        )

    def xa(self, d, o):
        p, sign = self.p, 1 - 2 * d
        return copy_to(
            self.part.at[p.zat(o), p.xat(sign)], self.la.at[d, o + 8],
            self.xs.at[d, o + 8], self.xr.at[d, o + 8], p.dev(0, sign),
        )

    def zc(self, o):
        p, i = self.p, o + 8
        ref, land, to = self.part.at[p.zat(o), p.x], self.lz.at[i], o
        if o not in NEAR and abs(o) != HUB:
            to = o - (HUB if o > 0 else -HUB)
            if abs(o) == 8:
                rows = self.half[0 if o > 0 else 1]
                ref, land = ref.at[rows, :], land.at[rows, :]
        return copy_to(ref, land, self.zs.at[i], self.zr.at[i], p.dev(to, 0))

    def ahead(self, o):
        for d in (0, 1):
            self.xh(d, o).start()

    def pass_x(self, o):
        p = self.p
        zz = p.zat(o)
        for d in (0, 1):
            self.xh(d, o).wait_recv()
            rows, xx = self.half[d], p.xat(1 - 2 * d)
            self.part[zz, xx, rows, :] = self.part[zz, xx, rows, :] + self.lh[d, o + 8]
            self.xa(d, o).start()

    def sum_x(self, o):
        p = self.p
        zz = p.zat(o)
        for d in (0, 1):
            self.xa(d, o).wait_recv()
        self.part[zz, p.x] = self.part[zz, p.x] + self.la[0, o + 8] + self.la[1, o + 8]
        if o == 8:
            self.zc(8).start()
            self.zc(-8).start()
        elif o and abs(o) != HUB:
            self.zc(o).start()

    def hub(self, o):
        p = self.p
        zz = p.zat(o)
        total = self.part[zz, p.x]
        for j in NEAR:
            self.zc(o + j).wait_recv()
            total = total + self.lz[o + j + 8]
        self.part[zz, p.x] = total
        i = 0 if o > 0 else 1
        end = 8 if o > 0 else -8
        self.zc(end).wait_recv()
        rows = self.half[i]
        self.part[zz, p.x, rows, :] = self.part[zz, p.x, rows, :] + self.lz[end + 8, rows, :]
        self.zc(o).start()

    def run(self, out, others):
        g = self.order
        lag = 3
        for o in g[:lag]:
            self.ahead(o)
        for i in range(len(g) + lag):
            if i + lag < len(g):
                self.ahead(g[i + lag])
            if i < len(g):
                self.pass_x(g[i])
            if i >= lag:
                self.sum_x(g[i - lag])
                if g[i - lag] == 1:
                    self.hub(HUB)
                if g[i - lag] == -1:
                    self.hub(-HUB)
            if i in others:
                others[i]()
        total = self.part[self.p.z, self.p.x]
        for o in NEAR + (HUB, -HUB):
            self.zc(o).wait_recv()
            total = total + self.lz[o + 8]
        out[...] = total
        for o in g:
            for d in (0, 1):
                self.xh(d, o).wait_send()
                self.xa(d, o).wait_send()
            if o:
                self.zc(o).wait_send()
        self.zc(-8).wait_send()


def rows_of(flat, at, n):
    return jnp.concatenate(
        [flat[pl.ds(at * NX + c, n, stride=NX), :] for c in range(RANK // LANE)], axis=1
    )


def to_flat(chunks, flat):
    c = chunks.shape[2]

    def body(i, _):
        flat[pl.ds(pl.multiple_of(i * c, 8), c), :] = chunks[i // NX, lax.rem(i, NX)]
        return _

    lax.fori_loop(0, chunks.shape[0] * NX, body, 0)


def w_rows(b_ref, l_ref, flat, cols):
    lh, ll = split2(l_ref[...])
    for j in range(0, cols, 256):
        w = dot3(b_ref[:, j : j + 256], (lh, ll), TN)
        for c in range(NX):
            flat[pl.ds(j * NX + c, 256, stride=NX), :] = w[:, c * LANE : (c + 1) * LANE]


def to_chunks(flat, part, c):
    def body(i, _):
        part[i // NX, lax.rem(i, NX)] = flat[pl.ds(pl.multiple_of(i * c, 8), c), :]
        return _

    lax.fori_loop(0, part.shape[0] * NX, body, 0)


def left_scratch(rows, nt):
    dma = pltpu.SemaphoreType.DMA
    return [pltpu.VMEM((rows, RANK), F32), pltpu.VMEM((nt, rows // nt, RANK), F32)] + [dma((nt,))] * 4


class Left:
    def __init__(self, nt, out, scratch):
        self.nt, self.out = nt, out
        self.t = lax.axis_index("tp")
        self.part, self.land, self.s1, self.r1, self.s2, self.r2 = scratch
        self.n = out.shape[0] // nt

    def peer(self, o):
        return lax.rem(self.t + o, self.nt)

    def piece(self, i):
        return pl.ds(pl.multiple_of(i * self.n, self.n), self.n)

    def out1(self, o):
        to = self.peer(o)
        return copy_to(self.part.at[self.piece(to), :], self.land.at[o],
                       self.s1.at[o], self.r1.at[o], {"tp": to})

    def out2(self, o):
        ref = self.out.at[self.piece(self.t), :]
        return copy_to(ref, ref, self.s2.at[o], self.r2.at[o], {"tp": self.peer(o)})

    def compute(self, blend, flat):
        acc = None
        for j in range(0, blend.shape[1], 256):
            d = dot3(blend[:, j : j + 256], rows_of(flat, j, 256), NN)
            acc = d if acc is None else acc + d
        self.part[...] = acc

    def run(self):
        for o in range(1, self.nt):
            self.out1(o).start()
        total = self.part[self.piece(self.t), :]
        for o in range(1, self.nt):
            self.out1(o).wait_recv()
            total = total + self.land[o]
        self.out[self.piece(self.t), :] = total
        for o in range(1, self.nt):
            self.out2(o).start()
        for o in range(1, self.nt):
            self.out2(o).wait_recv()

    def finish(self):
        for o in range(1, self.nt):
            self.out1(o).wait_send()
            self.out2(o).wait_send()


def gram_scratch(nz, nt):
    n = RANK // nt // NX
    dma = pltpu.SemaphoreType.DMA
    np_ = n * NX // 8
    return [
        pltpu.VMEM((RANK // nt, RANK), F32),
        pltpu.VMEM((NX, n, RANK), F32),
        pltpu.VMEM((n * NX, LANE), F32),
        pltpu.VMEM((nz, 8, LANE), F32),
        dma((NX,)), dma((NX,)),
        dma((nz,)), dma((nz,)),
        dma((np_,)), dma((np_,)),
        dma((NX,)), dma((NX,)),
        dma((nt,)), dma((nt,)),
    ]


class Gram:
    def __init__(self, place, nt, out, scratch):
        self.p, self.nt, self.out = place, nt, out
        (self.part, self.landx, self.flat, self.landz, self.s1, self.r1, self.s2, self.r2,
         self.s3, self.r3, self.s4, self.r4, self.s5, self.r5) = scratch
        self.t = lax.axis_index("tp")
        self.n = RANK // nt // NX
        self.pieces = self.n * NX // 8
        lo = -(self.pieces // 2)
        self.offs = [o for o in range(lo, lo + self.pieces) if o != 0]
        self.own = lax.rem(place.z, self.pieces)
        self.me = out.at[self.t, place.x]
        self.rows = pl.ds(pl.multiple_of(self.own * 8, 8), 8)

    def peer(self, o):
        return {"tp": lax.rem(self.t + o, self.nt)}

    def compute(self, l_ref):
        wide = RANK // self.nt
        col = pl.multiple_of(self.t * wide // LANE * LANE, LANE)
        full = dot3(l_ref[:, pl.ds(col, LANE)], l_ref[...], TN)
        which = lax.rem(self.t, LANE // wide)
        mine = full[0:wide]
        for i in range(1, LANE // wide):
            mine = jnp.where(which == i, full[i * wide : (i + 1) * wide], mine)
        self.part[...] = mine

    def c1(self, d):
        xx = self.p.xat(d)
        n = self.n
        return copy_to(self.part.at[pl.ds(pl.multiple_of(xx * n, n), n), :], self.landx.at[d],
                       self.s1.at[d], self.r1.at[d], self.p.dev(0, d))

    def c2(self, d):
        piece = lax.rem(self.p.zat(d), self.pieces)
        return copy_to(self.flat.at[pl.ds(pl.multiple_of(piece * 8, 8), 8), :],
                       self.landz.at[self.p.z], self.s2.at[d], self.r2.at[d], self.p.dev(d, 0))

    def c3(self, i):
        ref = self.me.at[self.rows, :]
        return copy_to(ref, ref, self.s3.at[i], self.r3.at[i], self.p.dev(self.offs[i], 0))

    def c4(self, d):
        return copy_to(self.me, self.me, self.s4.at[d], self.r4.at[d], self.p.dev(0, d))

    def c5(self, o):
        ref = self.out.at[self.t]
        return copy_to(ref, ref, self.s5.at[o], self.r5.at[o], self.peer(o))

    def stage1(self):
        for d in range(1, NX):
            self.c1(d).start()

    def stage2(self):
        n = self.n
        total = self.part[pl.ds(pl.multiple_of(self.p.x * n, n), n), :]
        for d in range(1, NX):
            self.c1(d).wait_recv()
            total = total + self.landx[d]
        for c in range(RANK // LANE):
            self.flat[pl.ds(c, n, stride=RANK // LANE), :] = total[:, c * LANE : (c + 1) * LANE]
        for d in range(1, self.p.nz):
            self.c2(d).start()
        self.landz[self.p.z] = self.flat[self.rows, :]

    def stage3(self):
        for d in range(1, self.p.nz):
            self.c2(d).wait_recv()
        tot = self.landz[0]
        for i in range(1, self.p.nz):
            tot = tot + self.landz[i]
        self.out[self.t, self.p.x, self.rows, :] = tot
        for i in range(len(self.offs)):
            self.c3(i).start()

    def stage4(self):
        for i in range(len(self.offs)):
            self.c3(i).wait_recv()
        for d in range(1, NX):
            self.c4(d).start()

    def stage5(self):
        for d in range(1, NX):
            self.c4(d).wait_recv()
        for o in range(1, self.nt):
            self.c5(o).start()

    def finish(self):
        for o in range(1, self.nt):
            self.c5(o).wait()
        for d in range(1, NX):
            self.c4(d).wait_send()
            self.c1(d).wait_send()
        for i in range(len(self.offs)):
            self.c3(i).wait_send()
        for d in range(1, self.p.nz):
            self.c2(d).wait_send()


BLOCK = 16


def split3(v):
    h = v.astype(BF16)
    r = v - h.astype(F32)
    m = r.astype(BF16)
    return h, m, (r - m.astype(F32)).astype(BF16)


def eliminate(a, at):
    n = a.shape[0]
    wide = a.shape[1] // LANE
    tiles = [a[:, i * LANE : (i + 1) * LANE] for i in range(wide)]
    d = [jnp.broadcast_to(a[:, at + k : at + k + 1], (n, LANE)) for k in range(n)]
    row = lax.broadcasted_iota(jnp.int32, (n, LANE), 0)
    scale = jnp.zeros((n, LANE), F32)
    for k in range(n):
        pivot = d[k][k : k + 1, :]
        r = lax.rsqrt(pivot)
        r = r * (1.5 - 0.5 * pivot * r * r)
        scale = jnp.where(row == k, r, scale)
        if k + 1 < n:
            f = jnp.where(row > k, d[k] * (r * r), 0.0)
            for m in range(k + 1, n):
                d[m] = d[m] - f * d[m][k : k + 1, :]
            tiles = [v - f * v[k : k + 1, :] for v in tiles]
    return jnp.concatenate([v * scale for v in tiles], axis=1)


def chol_panel(zz, p, between):
    wide = RANK + LANE
    c0 = pl.multiple_of(p * LANE, LANE)
    win = zz.at[pl.ds(c0, LANE), pl.ds(c0, wide)]
    for s in range(0, LANE, BLOCK):
        u = eliminate(win[s : s + BLOCK, :], s)
        win[s : s + BLOCK, :] = u
        if s + BLOCK < LANE:
            h, m, l = split3(u)
            lhs = jnp.concatenate([v[:, :LANE] for v in (h, h, m, h, l, m)], axis=0)
            rhs = jnp.concatenate([h, m, h, l, h, m], axis=0)
            upd = lax.dot_general(lhs, rhs, TN, preferred_element_type=F32)
            win[s + BLOCK :, :] = win[s + BLOCK :, :] - upd[s + BLOCK :, :]
        between(p, s // BLOCK)

    def below(i, _):
        at = pl.ds(pl.multiple_of(i * LANE, LANE), LANE)
        lhs = zz[pl.ds(c0, LANE), at]
        rest = pl.ds(pl.multiple_of(c0 + LANE, LANE), RANK)
        upd = lax.dot_general(lhs, zz[pl.ds(c0, LANE), rest], TN,
                              precision=lax.Precision.HIGHEST, preferred_element_type=F32)
        zz[at, rest] = zz[at, rest] - upd
        return _

    lax.fori_loop(p + 1, RANK // LANE, below, 0)


def chol_init(zz, g_ref):
    for c in range(RANK // LANE):
        zz[:, c * LANE : (c + 1) * LANE] = g_ref[pl.ds(c, RANK, stride=RANK // LANE), :]
    i = lax.broadcasted_iota(jnp.int32, (RANK, RANK), 0)
    j = lax.broadcasted_iota(jnp.int32, (RANK, RANK), 1)
    zz[:, RANK:] = jnp.where(i == j, 1.0, 0.0).astype(F32)


def last(nt, factor, m_ref, blend, left, x, own, flat, nm_ref, nb_ref, up_ref, scratch):
    wh, wl, sq, land, ss, rs = scratch
    t = lax.axis_index("tp")
    cols = blend.shape[1]
    x = split2(x)
    total = jnp.zeros((8, RANK), F32)
    for j in range(0, cols, 256):
        h, l = split2(rows_of(flat, j, 256))
        wh[j : j + 256, :] = h
        wl[j : j + 256, :] = l
        r = dot3((h, l), x, NT)
        total = total + jnp.sum((r * r).reshape(32, 8, RANK), axis=0)
    sq[...] = total

    def send(o):
        return copy_to(sq, land.at[o], ss.at[o], rs.at[o], {"tp": lax.rem(t + o, nt)})

    for o in range(1, nt):
        send(o).start()
    ortho = dot3(left, x, NT)
    m1 = split2(dot3(ortho, x, NN) * 0.1)
    right = dot3(rows_of(own, 0, own.shape[0] // NX), x, NT)
    for j in range(0, cols, 256):
        w = (wh[j : j + 256, :], wl[j : j + 256, :])
        nm_ref[:, j : j + 256] = blend[:, j : j + 256] - dot3(m1, w, NT)
    for o in range(1, nt):
        send(o).wait()
        total = total + land[o]
    inv = 1.0 / (jnp.sqrt(jnp.sum(total, axis=0, keepdims=True)) + 1e-06)
    nb_ref[...] = right * inv
    m2 = split2(dot3(ortho * (inv * factor), x, NN))
    for j in range(0, cols, 256):
        w = (wh[j : j + 256, :], wl[j : j + 256, :])
        up_ref[:, j : j + 256] = dot3(m2, w, NT).astype(BF16)


def last_scratch(cols, nt):
    dma = pltpu.SemaphoreType.DMA
    return [
        pltpu.VMEM((cols, RANK), BF16),
        pltpu.VMEM((cols, RANK), BF16),
        pltpu.VMEM((8, RANK), F32),
        pltpu.VMEM((nt, 8, RANK), F32),
        dma((nt,)), dma((nt,)),
    ]


def step_kernel(nz, nt, factor, m_ref, g_ref, q_ref, nm_ref, nb_ref, up_ref,
                blend, chunks, chunks2, flat, part, own, left_ref, gram_ref, zz, *scratch):
    scratch = list(scratch)

    def take(like):
        got = scratch[: len(like)]
        del scratch[: len(like)]
        return got

    rows, cols = m_ref.shape
    c = own.shape[0]
    place = Place(nz)
    gather = Gather(place, chunks, take(ag_sems()))
    left = Left(nt, left_ref, take(left_scratch(rows, nt)))
    gram = Gram(place, nt, gram_ref, take(gram_scratch(nz, nt)))
    scatter = Scatter(place, part, take(rs_scratch(c)))
    gather2 = Gather(place, chunks2, take(ag_sems()))
    lasts = take(last_scratch(cols, nt))

    for i in range(RANK // LANE):
        own[pl.ds(i, c // NX, stride=NX), :] = q_ref[:, i * LANE : (i + 1) * LANE]
    chunks[place.z, place.x] = own[...]
    greet(
        [place.dev(d, 0) for d in range(1, nz)]
        + [place.dev(0, d) for d in range(1, NX)]
        + [gram.peer(o) for o in range(1, nt)]
    )
    gather.begin()
    blend[...] = m_ref[...] + g_ref[...].astype(F32)
    for todo in gather.events():
        for f in todo:
            f()
    gather.finish()

    to_flat(chunks, flat)
    left.compute(blend, flat)
    left.run()
    gram.compute(left_ref)
    gram.stage1()
    left.finish()
    w_rows(blend, left_ref, flat, cols)
    to_chunks(flat, part, c)
    gram.stage2()
    scatter.run(own, {3: gram.stage3, 6: gram.stage4, 9: gram.stage5})
    chunks2[place.z, place.x] = own[...]
    gather2.begin()
    gram.finish()

    flat_gram(gram_ref, flat)
    chol_init(zz, flat)
    events = gather2.events()
    blocks = LANE // BLOCK

    def between(p, s):
        for pp in range(RANK // LANE):
            at = pp * blocks + s
            if at % 2 == 1 and at // 2 < len(events):

                @pl.when(p == pp)
                def _(at=at):
                    for f in events[at // 2]:
                        f()

    def body(p, _):
        chol_panel(zz, p, between)
        return _

    lax.fori_loop(0, RANK // LANE, body, 0)
    for todo in events[RANK // BLOCK // 2 :]:
        for f in todo:
            f()
    gather2.finish()
    to_flat(chunks2, flat)
    last(nt, factor, m_ref, blend, left_ref[...], zz[:, RANK:], own, flat,
         nm_ref, nb_ref, up_ref, lasts)


def flat_gram(gram_ref, flat):
    n = gram_ref.shape[2]

    def body(i, _):
        flat[pl.ds(pl.multiple_of(i * n, 8), n), :] = gram_ref[i // NX, lax.rem(i, NX)]
        return _

    lax.fori_loop(0, gram_ref.shape[0] * NX, body, 0)


def shards(nz, nt, factor, momentum, gradient, right_basis):
    rows, cols = momentum.shape
    n_own = right_basis.shape[0]
    c = n_own * RANK // LANE
    n = RANK // nt // NX
    return pl.pallas_call(
        functools.partial(step_kernel, nz, nt, factor),
        out_shape=(
            jax.ShapeDtypeStruct((rows, cols), F32),
            jax.ShapeDtypeStruct((n_own, RANK), F32),
            jax.ShapeDtypeStruct((rows, cols), BF16),
        ),
        in_specs=[VMEM] * 3,
        out_specs=(VMEM,) * 3,
        scratch_shapes=[
            pltpu.VMEM((rows, cols), F32),
            pltpu.VMEM((nz, NX, c, LANE), F32),
            pltpu.VMEM((nz, NX, c, LANE), F32),
            pltpu.VMEM((cols * RANK // LANE, LANE), F32),
            pltpu.VMEM((nz, NX, c, LANE), F32),
            pltpu.VMEM((c, LANE), F32),
            pltpu.VMEM((rows, RANK), F32),
            pltpu.VMEM((nt, NX, n * RANK // LANE, LANE), F32),
            pltpu.VMEM((RANK, 2 * RANK), F32),
        ]
        + ag_sems()
        + left_scratch(rows, nt)
        + gram_scratch(nz, nt)
        + rs_scratch(c)
        + ag_sems()
        + last_scratch(cols, nt),
        compiler_params=pltpu.CompilerParams(
            collective_id=1, has_side_effects=True, vmem_limit_bytes=56 << 20
        ),
    )(momentum, gradient, right_basis)


def solution(mesh):
    nz = mesh.shape["fsdp"] // NX
    nt = mesh.shape["tp"]
    factor = (float(ROWS) * COLS / RANK) ** 0.5
    placed = (P("fsdp", "tp"), P("fsdp", "tp"), P(("tp", "fsdp"), None))
    return jax.shard_map(
        functools.partial(shards, nz, nt, factor),
        mesh=mesh,
        in_specs=placed,
        out_specs=(P("fsdp", "tp"), P(("tp", "fsdp"), None), P("fsdp", "tp")),
        check_vma=False,
    )
```
